32 devices in a mesh: dp: 8 (over z, y), ctx: 4 (over x, core).
Axes of the slice: x: 2, y: 2, z: 4, core: 2. Of those that a mesh axis runs over, the one named last changes fastest.
Arguments:
- embeds: bfloat16 [8, 512, 4096], P('dp', 'ctx'), may hold values from -6 to 6
- norm_gain: float32 [4096], replicated, may hold values from 0.1 to 1.9
- w_key: bfloat16 [4096, 512], P('dp'), may hold values from -0.09375 to 0.09375
- w_value: bfloat16 [4096, 512], P('dp'), may hold values from -0.09375 to 0.09375
- queries: bfloat16 [8, 512, 4096], P('dp', 'ctx'), may hold values from -85 to 85
- d_out: bfloat16 [8, 512, 4096], P('dp', 'ctx'), may hold values from -6 to 6
- block_doc: int32 [8, 4], P('dp'), may hold values from 0 to 2, never falling along the last dimension, each value on 1 to 2 neighbouring positions
- slot_order: int32 [8, 8], P('dp'), may hold values from 0 to 7, each once within a row
Outputs:
- grad_embed: bfloat16 [8, 512, 4096], P('dp', 'ctx')
The draws below stay inside these ranges and needn't reach their ends.
Inputs may be any that keep to these rules, and one draw needn't show every extreme that they name: `block_doc`: along the blocks of a sequence the document number never falls; each of the 3 documents covers 1 to 2 blocks, and one covers exactly 2. `slot_order`: each row holds every number from 0 to 7 once.
All inputs are finite; a program needn't handle non-finite values.
Results may differ from the reference program's by a relative error of at most 0.035.
The reference program's roundings to bfloat16 on the way count: a program that leaves them out, or rounds other values in their place, can miss the bound.
Values may be sent and summed in bfloat16 or wider, within the bound.
A program may use at most 192 MiB of HBM per device.

```python
import math
import jax
import jax.numpy as jnp
import numpy as np
from jax import lax

D = 4096
HEADS = 32
KV_HEADS = 4
HEAD = 128
GROUP = 8
DOC_BLOCK = 128
BATCH = 8
SEQ = 512
HALF_TOK = 64
SLOTS = 8
NBLK = 4
NDOCS = 3
MOST_BLK = 2


def draw_queries(key, part):
    dims = (BATCH, SEQ, HEADS * HEAD)
    normal_part = jax.random.normal(key, dims, jnp.float32)
    return jnp.clip(normal_part, -6.0, 6.0).astype(jnp.bfloat16)


def block_levels(own_key, shape, shards, least, top_value):
    gain, own = 1.0, jax.random.fold_in(own_key, 6)
    for dim, blocks in shards:
        heights = jnp.exp(jax.random.uniform(jax.random.fold_in(own, dim), (blocks,), jnp.float32, least / len(shards), top_value / len(shards)))
        gain = gain * jnp.repeat(heights, shape[dim] // blocks).reshape([-1 if axis == dim else 1 for axis in range(len(shape))])
    return gain


def length_profile(count, total, bound, slope):
    portions = [(1 << 20) // math.isqrt(rank ** slope) + 1 for rank in range(2, count + 1)]
    spare, holding = total - bound - (count - 1), [1] * (count - 1)
    while spare > 0:
        candidates = [i for i in range(count - 1) if holding[i] < bound]
        mass, left = sum([portions[i] for i in candidates]), spare
        for i in candidates:
            addition = min(bound - holding[i], max(1, left * portions[i] // mass), spare)
            holding[i] = holding[i] + addition
            spare = spare - addition
    return np.array([bound] + holding)


def ragged_sizes(own_key, number_of, total, bound, lean):
    if number_of == 2:
        one = jax.random.randint(own_key, (), max(1, total - bound), min(bound, total - 1) + 1)
        return jnp.stack([one, total - one])
    lengths = jnp.asarray(length_profile(number_of, total, bound, lean), jnp.int32)
    couples = (number_of - 1) // 2
    giver, receiver = lengths[1:1 + 2 * couples:2], lengths[2:2 + 2 * couples:2]
    slack = jnp.minimum(giver - 1, bound - receiver)
    moved = jax.random.randint(jax.random.fold_in(own_key, 1), (couples,), 0, 1 << 20) % (slack + 1)
    lengths = lengths.at[1:1 + 2 * couples:2].set(giver - moved).at[2:2 + 2 * couples:2].set(receiver + moved)
    return lengths[jax.random.permutation(jax.random.fold_in(own_key, 2), number_of)]


def normal_values(key, shape, scale, reach, cuts=(), kind=jnp.bfloat16):
    array = scale * jax.random.normal(key, shape, jnp.float32)
    if cuts:
        array = array * block_levels(key, shape, cuts, -0.22, 0.18)
    return jnp.clip(array, -reach, reach).astype(kind)


def setup_inputs(seed: int = 0) -> dict:
    splits = jax.random.split(jax.random.key(seed), 9)
    embeds = normal_values(splits[0], (BATCH, SEQ, D), 1.0, 6.0, ((0, 8), (1, 4)))
    norm_gain = jnp.clip(1.0 + 0.18 * jax.random.normal(splits[1], (D,), jnp.float32), 0.1, 1.9)
    w_key = normal_values(splits[2], (D, KV_HEADS * HEAD), D ** -0.5, 0.09375, ((0, 8),))
    w_value = normal_values(splits[3], (D, KV_HEADS * HEAD), D ** -0.5, 0.09375, ((0, 8),))
    queries = draw_queries(jax.random.fold_in(splits[8], 71), 0)
    d_out = normal_values(splits[5], (BATCH, SEQ, HEADS * HEAD), 1.0, 6.0, ((0, 8), (1, 4)))
    block_doc = jax.vmap(lambda own: jnp.searchsorted(jnp.cumsum(ragged_sizes(own, NDOCS, NBLK, MOST_BLK, 1)), jnp.arange(NBLK), side="right"))(jax.random.split(splits[6], BATCH)).reshape((BATCH, NBLK)).astype(jnp.int32)
    slot_order = jax.vmap(lambda own: jax.random.permutation(own, SLOTS))(jax.random.split(splits[7], BATCH)).reshape((BATCH, SLOTS)).astype(jnp.int32)
    return dict(embeds=embeds, norm_gain=norm_gain, w_key=w_key, w_value=w_value, queries=queries, d_out=d_out, block_doc=block_doc, slot_order=slot_order)


def reference(embeds, norm_gain, w_key, w_value, queries, d_out, block_doc, slot_order):
    joined = jnp.concatenate([w_key, w_value], axis=1)
    kv_width = KV_HEADS * HEAD
    score_scale = HEAD ** (-0.5)

    def one_sequence(inputs):
        embed_rows, query_rows, dout_rows, doc_table, order_row = inputs
        row_ids = jnp.arange(SEQ, dtype=jnp.int32)
        position = (order_row[row_ids // HALF_TOK] * HALF_TOK + row_ids % HALF_TOK).astype(jnp.int32)
        document = doc_table[position // DOC_BLOCK]
        allowed = (position[None, :] <= position[:, None]) & (document[None, :] == document[:, None])
        as_float = embed_rows.astype(jnp.float32)
        inv_rms = lax.rsqrt(lax.optimization_barrier(jnp.mean(as_float * as_float, axis=-1, keepdims=True)) + 1e-05)
        normed = (as_float * inv_rms * norm_gain).astype(jnp.bfloat16)
        projected = jnp.dot(normed, joined, preferred_element_type=jnp.float32).astype(jnp.bfloat16)
        projected = lax.optimization_barrier(projected)
        key_grads = []
        value_grads = []
        for kv_head in range(KV_HEADS):
            first_col = kv_head * GROUP * HEAD
            last_col = (kv_head + 1) * GROUP * HEAD
            query_group = query_rows[:, first_col:last_col].reshape(SEQ, GROUP, HEAD).astype(jnp.float32)
            dout_group = dout_rows[:, first_col:last_col].reshape(SEQ, GROUP, HEAD).astype(jnp.float32)
            key_group = projected[:, kv_head * HEAD:(kv_head + 1) * HEAD].astype(jnp.float32)
            value_group = projected[:, kv_width + kv_head * HEAD:kv_width + (kv_head + 1) * HEAD].astype(jnp.float32)
            scores = jnp.einsum('thd,kd->htk', query_group, key_group) * score_scale
            row_max = lax.optimization_barrier(jnp.max(jnp.where(allowed[None], scores, -jnp.inf), axis=-1, keepdims=True))
            raised = jnp.where(allowed[None], jnp.exp(scores - row_max), 0.0)
            soft_probs = raised / lax.optimization_barrier(jnp.sum(raised, axis=-1, keepdims=True))
            probs_half = lax.optimization_barrier(soft_probs.astype(jnp.bfloat16)).astype(jnp.float32)
            attn_out = jnp.einsum('htk,kd->htd', probs_half, value_group)
            row_delta = jnp.einsum('htd,thd->ht', attn_out, dout_group)
            dprobs = jnp.einsum('thd,kd->htk', dout_group, value_group)
            score_grad = (soft_probs * (dprobs - row_delta[..., None]) * score_scale).astype(jnp.bfloat16)
            score_grad = lax.optimization_barrier(score_grad).astype(jnp.float32)
            key_grads.append(jnp.einsum('htk,thd->kd', score_grad, query_group))
            value_grads.append(jnp.einsum('htk,thd->kd', probs_half, dout_group))
        grad_half = jnp.concatenate(key_grads + value_grads, axis=1).astype(jnp.bfloat16)
        grad_normed = jnp.dot(grad_half, joined.T, preferred_element_type=jnp.float32)
        mean_term = lax.optimization_barrier(jnp.mean(as_float * norm_gain * grad_normed, axis=-1, keepdims=True))
        grad_embed = inv_rms * norm_gain * grad_normed - as_float * inv_rms * inv_rms * inv_rms * mean_term
        return grad_embed.astype(jnp.bfloat16)
    return lax.map(one_sequence, (embeds, queries, d_out, block_doc, slot_order))
```

```python
import functools
import math

import jax
import jax.numpy as jnp
from jax import lax
from jax.experimental import pallas as pl
from jax.experimental.pallas import tpu as pltpu
from jax.sharding import PartitionSpec as P

HEADS = 32
KV_HEADS = 4
HEAD = 128
GROUP = HEADS // KV_HEADS
DOC_BLOCK = 128
MESH = pl.DeviceIdType.MESH
F32 = jnp.float32
BF16 = jnp.bfloat16
NT = (((1,), (1,)), ((), ()))


def kernel(
    dp_ways,
    ctx_ways,
    wk_ref,
    wv_ref,
    emb_ref,
    gain_ref,
    q_ref,
    do_ref,
    bias_ref,
    out_ref,
    wg,
    wo,
    n2,
    kv,
    gs,
    rs,
    gn,
    dk_acc,
    dv_acc,
    w_send,
    w_recv,
    n_send,
    n_recv,
    wo_send,
    wo_recv,
    kv_send,
    kv_recv,
    g_send,
    g_recv,
):
    toks, dim = emb_ref.shape
    rows = dim // dp_ways
    line = dp_ways // 2
    chips = ctx_ways // 2
    splits = 2 if chips == 2 else 1
    part = rows // splits
    seq = toks * ctx_ways

    dp = lax.axis_index("dp")
    ctx = lax.axis_index("ctx")
    za, yb = dp // 2, dp % 2
    chip, core = ctx // 2, ctx % 2
    mine = chip % splits
    other = splits - 1 - mine
    partner = chip * 2 + 1 - core
    y_dp = za * 2 + 1 - yb
    x_ctx = (chips - 1 - chip) * 2 + core
    has_up, has_down = za + 1 < line, za >= 1
    sends = []

    def send(copy, cond=None):
        if cond is None:
            copy.start()
        else:
            pl.when(cond)(copy.start)
        sends.append((copy, cond))

    barrier = pltpu.get_barrier_semaphore()

    def greet(where):
        pl.semaphore_signal(barrier, inc=1, device_id=where, device_id_type=MESH)

    for step in range(1, ctx_ways):
        greet((dp, lax.rem(ctx + step, ctx_ways)))
    greet((y_dp, ctx))
    pl.when(has_up)(lambda: greet((dp + 2, ctx)))
    pl.when(has_down)(lambda: greet((dp - 2, ctx)))

    @pl.when(core == 0)
    def _():
        for h in range(KV_HEADS):
            wg[h, dp] = wk_ref[:, h * HEAD : (h + 1) * HEAD]

    @pl.when(core == 1)
    def _():
        for h in range(KV_HEADS):
            wg[h, dp] = wv_ref[:, h * HEAD : (h + 1) * HEAD]

    pl.semaphore_wait(
        barrier, ctx_ways + jnp.where(has_up, 1, 0) + jnp.where(has_down, 1, 0)
    )

    def piece(h, p, s):
        return wg.at[h, p, pl.ds(pl.multiple_of(s * part, part), part)]

    def w_copy(h, p, s, slot, where):
        return pltpu.make_async_remote_copy(
            src_ref=piece(h, p, s),
            dst_ref=piece(h, p, s),
            send_sem=w_send.at[h, p, slot],
            recv_sem=w_recv.at[h, p, s],
            device_id=where,
            device_id_type=MESH,
        )

    up, down, ybor, xbor = (dp + 2, ctx), (dp - 2, ctx), (y_dp, ctx), (dp, x_ctx)

    for h in range(KV_HEADS):
        send(w_copy(h, dp, mine, 0, up), has_up)
        send(w_copy(h, dp, mine, 1, down), has_down)
        send(w_copy(h, dp, mine, 2, ybor))
        if splits == 2:
            send(w_copy(h, dp, other, 3, ybor))

    step_cols = 512
    col_steps = dim // step_cols
    total = jnp.zeros((toks, 1), F32)
    for k in range(col_steps):
        e = emb_ref[:, k * step_cols : (k + 1) * step_cols].astype(F32)
        total += jnp.sum(e * e, axis=1, keepdims=True)
    inv_rms = lax.rsqrt(total * (1.0 / dim) + 1e-05)
    for k in range(col_steps):
        cols = slice(k * step_cols, (k + 1) * step_cols)
        e = emb_ref[:, cols].astype(F32)
        n2[core, :, cols] = (e * inv_rms * gain_ref[:, cols]).astype(BF16)
    n_copy = pltpu.make_async_remote_copy(
        src_ref=n2.at[core],
        dst_ref=n2.at[core],
        send_sem=n_send,
        recv_sem=n_recv,
        device_id=(dp, partner),
        device_id_type=MESH,
    )
    send(n_copy)

    def gather(h):
        for d in range(1, line):
            lo, hi = dp - 2 * d, dp + 2 * d
            lo_in, hi_in = za >= d, za + d < line

            @pl.when(lo_in)
            def _():
                w_copy(h, lo, mine, 0, up).wait_recv()

            send(w_copy(h, lo, mine, 0, up), lo_in & has_up)
            send(w_copy(h, lo, mine, 2, ybor), lo_in)
            if splits == 2:
                send(w_copy(h, lo, mine, 3, xbor), lo_in)

            @pl.when(hi_in)
            def _():
                w_copy(h, hi, mine, 0, up).wait_recv()

            send(w_copy(h, hi, mine, 1, down), hi_in & has_down)
            send(w_copy(h, hi, mine, 2, ybor), hi_in)
            if splits == 2:
                send(w_copy(h, hi, mine, 3, xbor), hi_in)
        w_copy(h, y_dp, mine, 0, up).wait_recv()
        if splits == 2:
            w_copy(h, y_dp, other, 0, up).wait_recv()
        for d in range(1, line):
            for far, inside in ((y_dp - 2 * d, za >= d), (y_dp + 2 * d, za + d < line)):

                @pl.when(inside)
                def _(far=far):
                    w_copy(h, far, mine, 0, up).wait_recv()

                if splits == 2:
                    send(w_copy(h, far, mine, 3, xbor), inside)
        if splits == 2:
            for d in range(1, line):
                for base in (dp, y_dp):
                    for far, inside in ((base - 2 * d, za >= d), (base + 2 * d, za + d < line)):

                        @pl.when(inside)
                        def _(far=far):
                            w_copy(h, far, other, 0, up).wait_recv()

    def project(h):
        acc = jnp.zeros((2 * toks, HEAD), F32)
        for p in range(dp_ways):
            x = n2[:, :, p * rows : (p + 1) * rows].reshape(2 * toks, rows)
            acc += jnp.dot(x, wg[h, p], preferred_element_type=F32)
        kv[core, h, pl.ds(chip * 2, 2)] = acc.astype(BF16).reshape(2, toks, HEAD)
        for step in range(1, ctx_ways):
            send(
                pltpu.make_async_remote_copy(
                    src_ref=kv.at[core, h, pl.ds(chip * 2, 2)],
                    dst_ref=kv.at[core, h, pl.ds(chip * 2, 2)],
                    send_sem=kv_send.at[h, step],
                    recv_sem=kv_recv.at[h, ctx],
                    device_id=(dp, lax.rem(ctx + step, ctx_ways)),
                    device_id_type=MESH,
                )
            )
        send(
            pltpu.make_async_remote_copy(
                src_ref=wg.at[h],
                dst_ref=wo.at[h],
                send_sem=wo_send.at[h],
                recv_sem=wo_recv.at[h],
                device_id=(dp, partner),
                device_id_type=MESH,
            )
        )

    wide = 2 if seq <= 512 else 1
    scale = HEAD ** (-0.5)

    def attend(h):
        for step in range(1, ctx_ways):
            src = lax.rem(ctx + step, ctx_ways)
            at = (src // 2) * 2
            blk = kv.at[src % 2, h, pl.ds(at, 2)]
            pltpu.make_async_remote_copy(
                src_ref=blk,
                dst_ref=blk,
                send_sem=kv_send.at[h, step],
                recv_sem=kv_recv.at[h, src],
                device_id=(dp, src),
                device_id_type=MESH,
            ).wait_recv()
        dk_acc[...] = jnp.zeros_like(dk_acc)
        dv_acc[...] = jnp.zeros_like(dv_acc)

        def chunk(i, carry):
            first = (h * GROUP + i * wide) * HEAD

            def take(ref):
                cuts = [
                    ref[:, pl.ds(pl.multiple_of(first + w * HEAD, HEAD), HEAD)]
                    for w in range(wide)
                ]
                return jnp.concatenate(cuts, axis=0) if wide > 1 else cuts[0]

            q, do = take(q_ref), take(do_ref)
            keys = kv[0, h].reshape(seq, HEAD)
            vals = kv[1, h].reshape(seq, HEAD)
            bias = bias_ref[...]
            if wide > 1:
                bias = jnp.concatenate([bias] * wide, axis=1)
            s = lax.dot_general(keys, q, NT, preferred_element_type=F32) + bias
            top = jnp.max(s, axis=0, keepdims=True)
            raised = jnp.exp2((s - top) * (scale * math.log2(math.e)))
            probs = raised * (1.0 / jnp.sum(raised, axis=0, keepdims=True))
            half = probs.astype(BF16)
            dpr = lax.dot_general(vals, do, NT, preferred_element_type=F32)
            delta = jnp.sum(half.astype(F32) * dpr, axis=0, keepdims=True)
            sg = (probs * (dpr - delta) * scale).astype(BF16)
            dk_acc[...] += jnp.dot(sg, q, preferred_element_type=F32)
            dv_acc[...] += jnp.dot(half, do, preferred_element_type=F32)
            return carry

        lax.fori_loop(0, GROUP // wide, chunk, 0)
        gs[h, :, 0] = dk_acc[...].astype(BF16).reshape(ctx_ways, toks, HEAD)
        gs[h, :, 1] = dv_acc[...].astype(BF16).reshape(ctx_ways, toks, HEAD)
        for step in range(1, ctx_ways):
            dst = lax.rem(ctx + step, ctx_ways)
            send(
                pltpu.make_async_remote_copy(
                    src_ref=gs.at[h, dst],
                    dst_ref=rs.at[h, ctx],
                    send_sem=g_send.at[h, step],
                    recv_sem=g_recv.at[h, ctx],
                    device_id=(dp, dst),
                    device_id_type=MESH,
                )
            )

    def backward(h):
        for step in range(1, ctx_ways):
            src = lax.rem(ctx + step, ctx_ways)
            pltpu.make_async_remote_copy(
                src_ref=gs.at[h, src],
                dst_ref=rs.at[h, src],
                send_sem=g_send.at[h, step],
                recv_sem=g_recv.at[h, src],
                device_id=(dp, src),
                device_id_type=MESH,
            ).wait_recv()
        pltpu.make_async_remote_copy(
            src_ref=wg.at[h],
            dst_ref=wo.at[h],
            send_sem=wo_send.at[h],
            recv_sem=wo_recv.at[h],
            device_id=(dp, partner),
            device_id_type=MESH,
        ).wait_recv()
        own = gs[h, ctx, core].astype(F32)
        cross = gs[h, ctx, 1 - core].astype(F32)
        for step in range(1, ctx_ways):
            src = lax.rem(ctx + step, ctx_ways)
            own += rs[h, src, core].astype(F32)
            cross += rs[h, src, 1 - core].astype(F32)
        own, cross = own.astype(BF16), cross.astype(BF16)
        for p in range(dp_ways):
            cols = slice(p * rows, (p + 1) * rows)
            term = lax.dot_general(own, wg[h, p], NT, preferred_element_type=F32)
            term += lax.dot_general(cross, wo[h, p], NT, preferred_element_type=F32)
            if h == 0:
                gn[:, cols] = term
            else:
                gn[:, cols] += term

    for h in range(KV_HEADS):
        gather(h)
        if h == 0:
            pltpu.make_async_remote_copy(
                src_ref=n2.at[1 - core],
                dst_ref=n2.at[1 - core],
                send_sem=n_send,
                recv_sem=n_recv,
                device_id=(dp, partner),
                device_id_type=MESH,
            ).wait_recv()
        project(h)
        if h >= 1:
            attend(h - 1)
        if h >= 2:
            backward(h - 2)
    attend(KV_HEADS - 1)
    if KV_HEADS >= 2:
        backward(KV_HEADS - 2)
    backward(KV_HEADS - 1)

    total = jnp.zeros((toks, 1), F32)
    for k in range(col_steps):
        cols = slice(k * step_cols, (k + 1) * step_cols)
        total += jnp.sum(
            emb_ref[:, cols].astype(F32) * gain_ref[:, cols] * gn[:, cols], axis=1, keepdims=True
        )
    shift = inv_rms * inv_rms * inv_rms * (total * (1.0 / dim))
    for k in range(col_steps):
        cols = slice(k * step_cols, (k + 1) * step_cols)
        e = emb_ref[:, cols].astype(F32)
        out_ref[:, cols] = (inv_rms * gain_ref[:, cols] * gn[:, cols] - e * shift).astype(BF16)

    for copy, cond in sends:
        if cond is None:
            copy.wait_send()
        else:
            pl.when(cond)(copy.wait_send)


def body(embeds, norm_gain, w_key, w_value, queries, d_out, block_doc, slot_order):
    embed_rows = embeds[0]
    toks, dim = embed_rows.shape
    dp_ways = lax.axis_size("dp")
    ctx_ways = lax.axis_size("ctx")
    seq = toks * ctx_ways
    half_len = seq // slot_order.shape[1]
    rows = dim // dp_ways
    row_ids = jnp.arange(seq, dtype=jnp.int32)
    slot_hit = (row_ids // half_len)[:, None] == jnp.arange(slot_order.shape[1], dtype=jnp.int32)
    pos = jnp.sum(jnp.where(slot_hit, slot_order[0][None, :], 0), axis=1) * half_len
    pos = pos + row_ids % half_len
    block_hit = (pos // DOC_BLOCK)[:, None] == jnp.arange(block_doc.shape[1], dtype=jnp.int32)
    doc = jnp.sum(jnp.where(block_hit, block_doc[0][None, :], 0), axis=1)
    start = lax.axis_index("ctx") * toks
    q_pos = lax.dynamic_slice_in_dim(pos, start, toks)
    q_doc = lax.dynamic_slice_in_dim(doc, start, toks)
    allowed = (pos[:, None] <= q_pos[None, :]) & (doc[:, None] == q_doc[None, :])
    bias = jnp.where(allowed, 0.0, -jnp.inf).astype(F32)

    vmem = pl.BlockSpec(memory_space=pltpu.VMEM)
    dma = pltpu.SemaphoreType.DMA
    splits = 2
    out = pl.pallas_call(
        functools.partial(kernel, dp_ways, ctx_ways),
        out_shape=jax.ShapeDtypeStruct((toks, dim), BF16),
        in_specs=[vmem] * 7,
        out_specs=vmem,
        scratch_shapes=[
            pltpu.VMEM((KV_HEADS, dp_ways, rows, HEAD), BF16),
            pltpu.VMEM((KV_HEADS, dp_ways, rows, HEAD), BF16),
            pltpu.VMEM((2, toks, dim), BF16),
            pltpu.VMEM((2, KV_HEADS, ctx_ways, toks, HEAD), BF16),
            pltpu.VMEM((KV_HEADS, ctx_ways, 2, toks, HEAD), BF16),
            pltpu.VMEM((KV_HEADS, ctx_ways, 2, toks, HEAD), BF16),
            pltpu.VMEM((toks, dim), F32),
            pltpu.VMEM((seq, HEAD), F32),
            pltpu.VMEM((seq, HEAD), F32),
            dma((KV_HEADS, dp_ways, 4)),
            dma((KV_HEADS, dp_ways, splits)),
            dma,
            dma,
            dma((KV_HEADS,)),
            dma((KV_HEADS,)),
            dma((KV_HEADS, ctx_ways)),
            dma((KV_HEADS, ctx_ways)),
            dma((KV_HEADS, ctx_ways)),
            dma((KV_HEADS, ctx_ways)),
        ],
        compiler_params=pltpu.CompilerParams(
            collective_id=0, has_side_effects=True, vmem_limit_bytes=56 * 1024 * 1024
        ),
    )(w_key, w_value, embed_rows, norm_gain[None], queries[0], d_out[0], bias)
    return out[None]


def solution(mesh):
    in_specs = (
        P("dp", "ctx", None),
        P(),
        P("dp", None),
        P("dp", None),
        P("dp", "ctx", None),
        P("dp", "ctx", None),
        P("dp", None),
        P("dp", None),
    )
    out_specs = P("dp", "ctx", None)
    return jax.shard_map(body, mesh=mesh, in_specs=in_specs, out_specs=out_specs, check_vma=False)
```

```python
import functools
import math

import jax
import jax.numpy as jnp
from jax import lax
from jax.experimental import pallas as pl
from jax.experimental.pallas import tpu as pltpu
from jax.sharding import PartitionSpec as P

HEADS = 32
KV_HEADS = 4
HEAD = 128
GROUP = HEADS // KV_HEADS
DOC_BLOCK = 128
MESH = pl.DeviceIdType.MESH
F32 = jnp.float32
BF16 = jnp.bfloat16
NT = (((1,), (1,)), ((), ()))


def kernel(
    dp_ways,
    ctx_ways,
    doc_ref,
    slot_ref,
    wk_hbm,
    wv_hbm,
    emb_hbm,
    gain_ref,
    q_hbm,
    do_hbm,
    out_ref,
    emb_ref,
    q_ref,
    do_ref,
    bias_ref,
    load_sem,
    own_sem,
    wg,
    wo,
    n2,
    kv,
    gs,
    rs,
    gn,
    dk_acc,
    dv_acc,
    w_send,
    w_recv,
    n_send,
    n_recv,
    wo_send,
    wo_recv,
    kv_send,
    kv_recv,
    g_send,
    g_recv,
):
    toks, dim = emb_hbm.shape
    rows = dim // dp_ways
    line = dp_ways // 2
    chips = ctx_ways // 2
    splits = 2 if chips == 2 else 1
    part = rows // splits
    seq = toks * ctx_ways

    dp = lax.axis_index("dp")
    ctx = lax.axis_index("ctx")
    za, yb = dp // 2, dp % 2
    chip, core = ctx // 2, ctx % 2
    mine = chip % splits
    other = splits - 1 - mine
    partner = chip * 2 + 1 - core
    y_dp = za * 2 + 1 - yb
    x_ctx = (chips - 1 - chip) * 2 + core
    has_up, has_down = za + 1 < line, za >= 1
    sends = []

    def send(copy, cond=None):
        if cond is None:
            copy.start()
        else:
            pl.when(cond)(copy.start)
        sends.append((copy, cond))

    barrier = pltpu.get_barrier_semaphore()

    def greet(where):
        pl.semaphore_signal(barrier, inc=1, device_id=where, device_id_type=MESH)

    for step in range(1, ctx_ways):
        greet((dp, lax.rem(ctx + step, ctx_ways)))
    greet((y_dp, ctx))
    pl.when(has_up)(lambda: greet((dp + 2, ctx)))
    pl.when(has_down)(lambda: greet((dp - 2, ctx)))

    def own_load(src, h):
        return pltpu.make_async_copy(
            src.at[:, pl.ds(h * HEAD, HEAD)], wg.at[h, dp], own_sem.at[h]
        )

    for h in range(KV_HEADS):
        pl.when(core == 0)(own_load(wk_hbm, h).start)
        pl.when(core == 1)(own_load(wv_hbm, h).start)
    loads = [
        pltpu.make_async_copy(src, dst, load_sem.at[i])
        for i, (src, dst) in enumerate(((emb_hbm, emb_ref), (q_hbm, q_ref), (do_hbm, do_ref)))
    ]
    for load in loads:
        load.start()

    pl.semaphore_wait(
        barrier, ctx_ways + jnp.where(has_up, 1, 0) + jnp.where(has_down, 1, 0)
    )

    up, down, ybor, xbor = (dp + 2, ctx), (dp - 2, ctx), (y_dp, ctx), (dp, x_ctx)

    def w_copy(h, p, s, slot, where):
        if s is None:
            ref, sem = wg.at[h, p], 0
        else:
            ref, sem = wg.at[h, p, pl.ds(pl.multiple_of(s * part, part), part)], s
        return pltpu.make_async_remote_copy(
            src_ref=ref,
            dst_ref=ref,
            send_sem=w_send.at[h, p, slot],
            recv_sem=w_recv.at[h, p, sem],
            device_id=where,
            device_id_type=MESH,
        )

    def arrive(h, p, s, cond):
        @pl.when(cond)
        def _():
            w_copy(h, p, s, 0, up).wait_recv()

    def start_own(h):
        own_load(wk_hbm, h).wait()
        send(w_copy(h, dp, None, 0, up), has_up)
        send(w_copy(h, dp, None, 1, down), has_down)
        send(w_copy(h, dp, None, 2, ybor))

    def sides(d):
        odd = za % 2 == 1
        never = za < 0
        return (
            (-2 * d, za >= d, odd if d == 1 else never, 1),
            (2 * d, za + d < line, jnp.logical_not(odd) if d == 1 else never, 0),
        )

    def relay(h, k):
        if k < line:
            for off, inside, whole, away in sides(k):
                p = dp + off
                arrive(h, p, None, inside)
                if away == 1:
                    send(w_copy(h, p, None, 0, up), inside & has_up)
                else:
                    send(w_copy(h, p, None, 1, down), inside & has_down)
                if splits == 1:
                    send(w_copy(h, p, None, 2, ybor), inside)
                else:
                    if k == 1:
                        send(w_copy(h, p, None, 2, ybor), inside & whole)
                    send(
                        w_copy(h, p, mine, 2, ybor),
                        inside & jnp.logical_not(whole) if k == 1 else inside,
                    )
        if k > 1 and splits == 2:
            for off, inside, whole, _away in sides(k - 1):
                p = y_dp + off
                half = inside & jnp.logical_not(whole) if k == 2 else inside
                arrive(h, p, mine, half)
                send(w_copy(h, p, mine, 3, xbor), half)

    def complete(h):
        w_copy(h, y_dp, None, 0, up).wait_recv()
        for d in range(1, line):
            for off, inside, whole, _away in sides(d):
                p = y_dp + off
                if splits == 1:
                    arrive(h, p, None, inside)
                elif d == 1:
                    arrive(h, p, None, inside & whole)
                    arrive(h, p, other, inside & jnp.logical_not(whole))
                else:
                    arrive(h, p, other, inside)

    def wave(w):
        if w + 1 < KV_HEADS:
            start_own(w + 1)
        for h in range(KV_HEADS):
            if 1 <= w - h + 1 <= line:
                relay(h, w - h + 1)

    start_own(0)
    loads[0].wait()

    step_cols = 512
    col_steps = dim // step_cols
    total = jnp.zeros((toks, 1), F32)
    for k in range(col_steps):
        e = emb_ref[:, k * step_cols : (k + 1) * step_cols].astype(F32)
        total += jnp.sum(e * e, axis=1, keepdims=True)
    inv_rms = lax.rsqrt(total * (1.0 / dim) + 1e-05)
    wave(0)
    for k in range(col_steps):
        cols = slice(k * step_cols, (k + 1) * step_cols)
        e = emb_ref[:, cols].astype(F32)
        n2[core, :, cols] = (e * inv_rms * gain_ref[:, cols]).astype(BF16)
    n_copy = pltpu.make_async_remote_copy(
        src_ref=n2.at[core],
        dst_ref=n2.at[core],
        send_sem=n_send,
        recv_sem=n_recv,
        device_id=(dp, partner),
        device_id_type=MESH,
    )
    send(n_copy)

    slots = slot_ref.shape[1]
    half_len = seq // slots
    lane = lax.broadcasted_iota(jnp.int32, (1, toks), 1)
    down_rows = lax.broadcasted_iota(jnp.int32, (half_len, 1), 0)
    per_dev = toks // half_len

    def slot_doc(start):
        block, found = start // DOC_BLOCK, jnp.int32(0)
        for i in range(doc_ref.shape[1]):
            found = jnp.where(block == i, doc_ref[0, i], found)
        return found

    q_pos = jnp.zeros((1, toks), jnp.int32)
    q_doc = jnp.zeros((1, toks), jnp.int32)
    for i in range(per_dev):
        start = slot_ref[0, ctx * per_dev + i] * half_len
        here = (lane >= i * half_len) & (lane < (i + 1) * half_len)
        q_pos = jnp.where(here, start + lane - i * half_len, q_pos)
        q_doc = jnp.where(here, slot_doc(start), q_doc)
    for j in range(slots):
        start = slot_ref[0, j] * half_len
        allowed = ((start + down_rows) <= q_pos) & (q_doc == slot_doc(start))
        bias_ref[j * half_len : (j + 1) * half_len, :] = jnp.where(allowed, 0.0, -jnp.inf)

    def project(h):
        acc = jnp.zeros((2 * toks, HEAD), F32)
        for p in range(dp_ways):
            x = n2[:, :, p * rows : (p + 1) * rows].reshape(2 * toks, rows)
            acc += jnp.dot(x, wg[h, p], preferred_element_type=F32)
        kv[core, h, pl.ds(chip * 2, 2)] = acc.astype(BF16).reshape(2, toks, HEAD)
        for step in range(1, ctx_ways):
            send(
                pltpu.make_async_remote_copy(
                    src_ref=kv.at[core, h, pl.ds(chip * 2, 2)],
                    dst_ref=kv.at[core, h, pl.ds(chip * 2, 2)],
                    send_sem=kv_send.at[h, step],
                    recv_sem=kv_recv.at[h, ctx],
                    device_id=(dp, lax.rem(ctx + step, ctx_ways)),
                    device_id_type=MESH,
                )
            )
        send(
            pltpu.make_async_remote_copy(
                src_ref=wg.at[h],
                dst_ref=wo.at[h],
                send_sem=wo_send.at[h],
                recv_sem=wo_recv.at[h],
                device_id=(dp, partner),
                device_id_type=MESH,
            )
        )

    wide = 2 if seq <= 512 else 1
    scale = HEAD ** (-0.5)

    def attend(h, between=None):
        for step in range(1, ctx_ways):
            src = lax.rem(ctx + step, ctx_ways)
            at = (src // 2) * 2
            blk = kv.at[src % 2, h, pl.ds(at, 2)]
            pltpu.make_async_remote_copy(
                src_ref=blk,
                dst_ref=blk,
                send_sem=kv_send.at[h, step],
                recv_sem=kv_recv.at[h, src],
                device_id=(dp, src),
                device_id_type=MESH,
            ).wait_recv()
        dk_acc[...] = jnp.zeros_like(dk_acc)
        dv_acc[...] = jnp.zeros_like(dv_acc)
        if h == 0:
            loads[1].wait()
            loads[2].wait()

        def chunk(i, carry):
            first = (h * GROUP + i * wide) * HEAD

            def take(ref):
                cuts = [
                    ref[:, pl.ds(pl.multiple_of(first + w * HEAD, HEAD), HEAD)]
                    for w in range(wide)
                ]
                return jnp.concatenate(cuts, axis=0) if wide > 1 else cuts[0]

            q, do = take(q_ref), take(do_ref)
            keys = kv[0, h].reshape(seq, HEAD)
            vals = kv[1, h].reshape(seq, HEAD)
            bias = bias_ref[...]
            if wide > 1:
                bias = jnp.concatenate([bias] * wide, axis=1)
            s = lax.dot_general(keys, q, NT, preferred_element_type=F32) + bias
            top = jnp.max(s, axis=0, keepdims=True)
            raised = jnp.exp2((s - top) * (scale * math.log2(math.e)))
            probs = raised * (1.0 / jnp.sum(raised, axis=0, keepdims=True))
            half = probs.astype(BF16)
            dpr = lax.dot_general(vals, do, NT, preferred_element_type=F32)
            delta = jnp.sum(half.astype(F32) * dpr, axis=0, keepdims=True)
            sg = (probs * (dpr - delta) * scale).astype(BF16)
            dk_acc[...] += jnp.dot(sg, q, preferred_element_type=F32)
            dv_acc[...] += jnp.dot(half, do, preferred_element_type=F32)
            return carry

        cut = GROUP // wide // 2
        lax.fori_loop(0, cut, chunk, 0)
        if between is not None:
            between()
        lax.fori_loop(cut, GROUP // wide, chunk, 0)
        gs[h, :, 0] = dk_acc[...].astype(BF16).reshape(ctx_ways, toks, HEAD)
        gs[h, :, 1] = dv_acc[...].astype(BF16).reshape(ctx_ways, toks, HEAD)
        for step in range(1, ctx_ways):
            dst = lax.rem(ctx + step, ctx_ways)
            send(
                pltpu.make_async_remote_copy(
                    src_ref=gs.at[h, dst],
                    dst_ref=rs.at[h, ctx],
                    send_sem=g_send.at[h, step],
                    recv_sem=g_recv.at[h, ctx],
                    device_id=(dp, dst),
                    device_id_type=MESH,
                )
            )

    def backward(h):
        for step in range(1, ctx_ways):
            src = lax.rem(ctx + step, ctx_ways)
            pltpu.make_async_remote_copy(
                src_ref=gs.at[h, src],
                dst_ref=rs.at[h, src],
                send_sem=g_send.at[h, step],
                recv_sem=g_recv.at[h, src],
                device_id=(dp, src),
                device_id_type=MESH,
            ).wait_recv()
        pltpu.make_async_remote_copy(
            src_ref=wg.at[h],
            dst_ref=wo.at[h],
            send_sem=wo_send.at[h],
            recv_sem=wo_recv.at[h],
            device_id=(dp, partner),
            device_id_type=MESH,
        ).wait_recv()
        own = gs[h, ctx, core].astype(F32)
        cross = gs[h, ctx, 1 - core].astype(F32)
        for step in range(1, ctx_ways):
            src = lax.rem(ctx + step, ctx_ways)
            own += rs[h, src, core].astype(F32)
            cross += rs[h, src, 1 - core].astype(F32)
        own, cross = own.astype(BF16), cross.astype(BF16)
        for p in range(dp_ways):
            cols = slice(p * rows, (p + 1) * rows)
            term = lax.dot_general(own, wg[h, p], NT, preferred_element_type=F32)
            term += lax.dot_general(cross, wo[h, p], NT, preferred_element_type=F32)
            if h == 0:
                gn[:, cols] = term
            else:
                gn[:, cols] += term

    for w in range(1, line + 1):
        wave(w)
    complete(0)
    pltpu.make_async_remote_copy(
        src_ref=n2.at[1 - core],
        dst_ref=n2.at[1 - core],
        send_sem=n_send,
        recv_sem=n_recv,
        device_id=(dp, partner),
        device_id_type=MESH,
    ).wait_recv()
    for h in range(KV_HEADS):
        if h > 0:
            complete(h)
        project(h)
        if h >= 2:
            backward(h - 2)
        attend(h, functools.partial(wave, line + 1 + h))
    backward(KV_HEADS - 2)
    backward(KV_HEADS - 1)

    total = jnp.zeros((toks, 1), F32)
    for k in range(col_steps):
        cols = slice(k * step_cols, (k + 1) * step_cols)
        total += jnp.sum(
            emb_ref[:, cols].astype(F32) * gain_ref[:, cols] * gn[:, cols], axis=1, keepdims=True
        )
    shift = inv_rms * inv_rms * inv_rms * (total * (1.0 / dim))
    for k in range(col_steps):
        cols = slice(k * step_cols, (k + 1) * step_cols)
        e = emb_ref[:, cols].astype(F32)
        out_ref[:, cols] = (inv_rms * gain_ref[:, cols] * gn[:, cols] - e * shift).astype(BF16)

    for copy, cond in sends:
        if cond is None:
            copy.wait_send()
        else:
            pl.when(cond)(copy.wait_send)


def body(embeds, norm_gain, w_key, w_value, queries, d_out, block_doc, slot_order):
    embed_rows = embeds[0]
    toks, dim = embed_rows.shape
    dp_ways = lax.axis_size("dp")
    ctx_ways = lax.axis_size("ctx")
    seq = toks * ctx_ways
    rows = dim // dp_ways
    vmem = pl.BlockSpec(memory_space=pltpu.VMEM)
    smem = pl.BlockSpec(memory_space=pltpu.SMEM)
    hbm = pl.BlockSpec(memory_space=pl.ANY)
    dma = pltpu.SemaphoreType.DMA
    splits = 2
    out = pl.pallas_call(
        functools.partial(kernel, dp_ways, ctx_ways),
        out_shape=jax.ShapeDtypeStruct((toks, dim), BF16),
        in_specs=[smem, smem, hbm, hbm, hbm, vmem, hbm, hbm],
        out_specs=vmem,
        scratch_shapes=[
            pltpu.VMEM((toks, dim), BF16),
            pltpu.VMEM((toks, dim), BF16),
            pltpu.VMEM((toks, dim), BF16),
            pltpu.VMEM((seq, toks), F32),
            dma((3,)),
            dma((KV_HEADS,)),
            pltpu.VMEM((KV_HEADS, dp_ways, rows, HEAD), BF16),
            pltpu.VMEM((KV_HEADS, dp_ways, rows, HEAD), BF16),
            pltpu.VMEM((2, toks, dim), BF16),
            pltpu.VMEM((2, KV_HEADS, ctx_ways, toks, HEAD), BF16),
            pltpu.VMEM((KV_HEADS, ctx_ways, 2, toks, HEAD), BF16),
            pltpu.VMEM((KV_HEADS, ctx_ways, 2, toks, HEAD), BF16),
            pltpu.VMEM((toks, dim), F32),
            pltpu.VMEM((seq, HEAD), F32),
            pltpu.VMEM((seq, HEAD), F32),
            dma((KV_HEADS, dp_ways, 4)),
            dma((KV_HEADS, dp_ways, splits)),
            dma,
            dma,
            dma((KV_HEADS,)),
            dma((KV_HEADS,)),
            dma((KV_HEADS, ctx_ways)),
            dma((KV_HEADS, ctx_ways)),
            dma((KV_HEADS, ctx_ways)),
            dma((KV_HEADS, ctx_ways)),
        ],
        compiler_params=pltpu.CompilerParams(
            collective_id=0, has_side_effects=True, vmem_limit_bytes=56 * 1024 * 1024
        ),
    )(
        block_doc, slot_order, w_key, w_value, embed_rows, norm_gain[None], queries[0], d_out[0]
    )
    return out[None]


def solution(mesh):
    in_specs = (
        P("dp", "ctx", None),
        P(),
        P("dp", None),
        P("dp", None),
        P("dp", "ctx", None),
        P("dp", "ctx", None),
        P("dp", None),
        P("dp", None),
    )
    out_specs = P("dp", "ctx", None)
    return jax.shard_map(body, mesh=mesh, in_specs=in_specs, out_specs=out_specs, check_vma=False)
```

```python
import functools
import math

import jax
import jax.numpy as jnp
from jax import lax
from jax.experimental import pallas as pl
from jax.experimental.pallas import tpu as pltpu
from jax.sharding import PartitionSpec as P

HEADS = 32
KV_HEADS = 4
HEAD = 128
GROUP = HEADS // KV_HEADS
DOC_BLOCK = 128
MESH = pl.DeviceIdType.MESH
F32 = jnp.float32
BF16 = jnp.bfloat16
NT = (((1,), (1,)), ((), ()))


def kernel(
    dp_ways,
    ctx_ways,
    doc_ref,
    slot_ref,
    wk_hbm,
    wv_hbm,
    emb_hbm,
    gain_ref,
    q_hbm,
    do_hbm,
    out_ref,
    emb_ref,
    q_ref,
    do_ref,
    bias_ref,
    load_sem,
    own_sem,
    wg,
    wo,
    n2,
    kv,
    gs,
    rs,
    gn,
    dk_acc,
    dv_acc,
    w_send,
    w_recv,
    n_send,
    n_recv,
    wo_send,
    wo_recv,
    kv_send,
    kv_recv,
    g_send,
    g_recv,
):
    toks, dim = emb_hbm.shape
    rows = dim // dp_ways
    line = dp_ways // 2
    chips = ctx_ways // 2
    splits = 2 if chips == 2 else 1
    part = rows // splits
    seq = toks * ctx_ways

    dp = lax.axis_index("dp")
    ctx = lax.axis_index("ctx")
    za, yb = dp // 2, dp % 2
    chip, core = ctx // 2, ctx % 2
    mine = chip % splits
    other = splits - 1 - mine
    partner = chip * 2 + 1 - core
    y_dp = za * 2 + 1 - yb
    x_ctx = (chips - 1 - chip) * 2 + core
    has_up, has_down = za + 1 < line, za >= 1
    sends = []

    def send(copy, cond=None):
        if cond is None:
            copy.start()
        else:
            pl.when(cond)(copy.start)
        sends.append((copy, cond))

    barrier = pltpu.get_barrier_semaphore()

    def greet(where):
        pl.semaphore_signal(barrier, inc=1, device_id=where, device_id_type=MESH)

    for step in range(1, ctx_ways):
        greet((dp, lax.rem(ctx + step, ctx_ways)))
    greet((y_dp, ctx))
    pl.when(has_up)(lambda: greet((dp + 2, ctx)))
    pl.when(has_down)(lambda: greet((dp - 2, ctx)))

    def own_load(src, h):
        return pltpu.make_async_copy(
            src.at[:, pl.ds(h * HEAD, HEAD)], wg.at[h, dp], own_sem.at[h]
        )

    for h in range(KV_HEADS):
        pl.when(core == 0)(own_load(wk_hbm, h).start)
        pl.when(core == 1)(own_load(wv_hbm, h).start)
    loads = [
        pltpu.make_async_copy(src, dst, load_sem.at[i])
        for i, (src, dst) in enumerate(((emb_hbm, emb_ref), (q_hbm, q_ref), (do_hbm, do_ref)))
    ]
    for load in loads:
        load.start()

    pl.semaphore_wait(
        barrier, ctx_ways + jnp.where(has_up, 1, 0) + jnp.where(has_down, 1, 0)
    )

    up, down, ybor, xbor = (dp + 2, ctx), (dp - 2, ctx), (y_dp, ctx), (dp, x_ctx)

    def w_copy(h, p, s, slot, where):
        if s is None:
            ref, sem = wg.at[h, p], 0
        else:
            ref, sem = wg.at[h, p, pl.ds(pl.multiple_of(s * part, part), part)], s
        return pltpu.make_async_remote_copy(
            src_ref=ref,
            dst_ref=ref,
            send_sem=w_send.at[h, p, slot],
            recv_sem=w_recv.at[h, p, sem],
            device_id=where,
            device_id_type=MESH,
        )

    def arrive(h, p, s, cond):
        @pl.when(cond)
        def _():
            w_copy(h, p, s, 0, up).wait_recv()

    def start_own(h):
        own_load(wk_hbm, h).wait()
        send(w_copy(h, dp, None, 0, up), has_up)
        send(w_copy(h, dp, None, 1, down), has_down)
        send(w_copy(h, dp, None, 2, ybor))

    def sides(d):
        odd = za % 2 == 1
        never = za < 0
        return (
            (-2 * d, za >= d, odd if d == 1 else never, 1),
            (2 * d, za + d < line, jnp.logical_not(odd) if d == 1 else never, 0),
        )

    def relay(h, k):
        if k < line:
            for off, inside, whole, away in sides(k):
                p = dp + off
                arrive(h, p, None, inside)
                if away == 1:
                    send(w_copy(h, p, None, 0, up), inside & has_up)
                else:
                    send(w_copy(h, p, None, 1, down), inside & has_down)
                if splits == 1:
                    send(w_copy(h, p, None, 2, ybor), inside)
                else:
                    if k == 1:
                        send(w_copy(h, p, None, 2, ybor), inside & whole)
                    send(
                        w_copy(h, p, mine, 2, ybor),
                        inside & jnp.logical_not(whole) if k == 1 else inside,
                    )
        if k > 1 and splits == 2:
            for off, inside, whole, _away in sides(k - 1):
                p = y_dp + off
                half = inside & jnp.logical_not(whole) if k == 2 else inside
                arrive(h, p, mine, half)
                send(w_copy(h, p, mine, 3, xbor), half)

    def complete(h):
        w_copy(h, y_dp, None, 0, up).wait_recv()
        for d in range(1, line):
            for off, inside, whole, _away in sides(d):
                p = y_dp + off
                if splits == 1:
                    arrive(h, p, None, inside)
                elif d == 1:
                    arrive(h, p, None, inside & whole)
                    arrive(h, p, other, inside & jnp.logical_not(whole))
                else:
                    arrive(h, p, other, inside)

    steps = [
        (h, w - h + 1)
        for w in range(KV_HEADS + line - 1)
        for h in range(KV_HEADS)
        if 1 <= w - h + 1 <= line
    ]

    def relays(count):
        for _ in range(min(count, len(steps))):
            h, k = steps.pop(0)
            if k == 1 and h + 1 < KV_HEADS:
                start_own(h + 1)
            relay(h, k)

    def relays_through(h):
        if (h, line) in steps:
            relays(steps.index((h, line)) + 1)

    start_own(0)
    loads[0].wait()

    step_cols = 512
    col_steps = dim // step_cols
    total = jnp.zeros((toks, 1), F32)
    for k in range(col_steps):
        e = emb_ref[:, k * step_cols : (k + 1) * step_cols].astype(F32)
        total += jnp.sum(e * e, axis=1, keepdims=True)
    inv_rms = lax.rsqrt(total * (1.0 / dim) + 1e-05)
    relays(1)
    for k in range(col_steps):
        cols = slice(k * step_cols, (k + 1) * step_cols)
        e = emb_ref[:, cols].astype(F32)
        n2[core, :, cols] = (e * inv_rms * gain_ref[:, cols]).astype(BF16)
    n_copy = pltpu.make_async_remote_copy(
        src_ref=n2.at[core],
        dst_ref=n2.at[core],
        send_sem=n_send,
        recv_sem=n_recv,
        device_id=(dp, partner),
        device_id_type=MESH,
    )
    send(n_copy)

    slots = slot_ref.shape[1]
    half_len = seq // slots
    lane = lax.broadcasted_iota(jnp.int32, (1, toks), 1)
    down_rows = lax.broadcasted_iota(jnp.int32, (half_len, 1), 0)
    per_dev = toks // half_len

    def slot_doc(start):
        block, found = start // DOC_BLOCK, jnp.int32(0)
        for i in range(doc_ref.shape[1]):
            found = jnp.where(block == i, doc_ref[0, i], found)
        return found

    q_pos = jnp.zeros((1, toks), jnp.int32)
    q_doc = jnp.zeros((1, toks), jnp.int32)
    for i in range(per_dev):
        start = slot_ref[0, ctx * per_dev + i] * half_len
        here = (lane >= i * half_len) & (lane < (i + 1) * half_len)
        q_pos = jnp.where(here, start + lane - i * half_len, q_pos)
        q_doc = jnp.where(here, slot_doc(start), q_doc)
    for j in range(slots):
        start = slot_ref[0, j] * half_len
        allowed = ((start + down_rows) <= q_pos) & (q_doc == slot_doc(start))
        bias_ref[j * half_len : (j + 1) * half_len, :] = jnp.where(allowed, 0.0, -jnp.inf)

    def project(h):
        acc = jnp.zeros((2 * toks, HEAD), F32)
        for p in range(dp_ways):
            x = n2[:, :, p * rows : (p + 1) * rows].reshape(2 * toks, rows)
            acc += jnp.dot(x, wg[h, p], preferred_element_type=F32)
        kv[core, h, pl.ds(chip * 2, 2)] = acc.astype(BF16).reshape(2, toks, HEAD)
        for step in range(1, ctx_ways):
            send(
                pltpu.make_async_remote_copy(
                    src_ref=kv.at[core, h, pl.ds(chip * 2, 2)],
                    dst_ref=kv.at[core, h, pl.ds(chip * 2, 2)],
                    send_sem=kv_send.at[h, step],
                    recv_sem=kv_recv.at[h, ctx],
                    device_id=(dp, lax.rem(ctx + step, ctx_ways)),
                    device_id_type=MESH,
                )
            )
        send(
            pltpu.make_async_remote_copy(
                src_ref=wg.at[h],
                dst_ref=wo.at[h],
                send_sem=wo_send.at[h],
                recv_sem=wo_recv.at[h],
                device_id=(dp, partner),
                device_id_type=MESH,
            )
        )

    wide = 2 if seq <= 512 else 1
    scale = HEAD ** (-0.5)

    def attend(h, between=None):
        for step in range(1, ctx_ways):
            src = lax.rem(ctx + step, ctx_ways)
            at = (src // 2) * 2
            blk = kv.at[src % 2, h, pl.ds(at, 2)]
            pltpu.make_async_remote_copy(
                src_ref=blk,
                dst_ref=blk,
                send_sem=kv_send.at[h, step],
                recv_sem=kv_recv.at[h, src],
                device_id=(dp, src),
                device_id_type=MESH,
            ).wait_recv()
        dk_acc[...] = jnp.zeros_like(dk_acc)
        dv_acc[...] = jnp.zeros_like(dv_acc)
        if h == 0:
            loads[1].wait()
            loads[2].wait()

        def chunk(i, carry):
            first = (h * GROUP + i * wide) * HEAD

            def take(ref):
                cuts = [
                    ref[:, pl.ds(pl.multiple_of(first + w * HEAD, HEAD), HEAD)]
                    for w in range(wide)
                ]
                return jnp.concatenate(cuts, axis=0) if wide > 1 else cuts[0]

            q, do = take(q_ref), take(do_ref)
            keys = kv[0, h].reshape(seq, HEAD)
            vals = kv[1, h].reshape(seq, HEAD)
            bias = bias_ref[...]
            if wide > 1:
                bias = jnp.concatenate([bias] * wide, axis=1)
            s = lax.dot_general(keys, q, NT, preferred_element_type=F32) + bias
            top = jnp.max(s, axis=0, keepdims=True)
            raised = jnp.exp2((s - top) * (scale * math.log2(math.e)))
            probs = raised * (1.0 / jnp.sum(raised, axis=0, keepdims=True))
            half = probs.astype(BF16)
            dpr = lax.dot_general(vals, do, NT, preferred_element_type=F32)
            delta = jnp.sum(half.astype(F32) * dpr, axis=0, keepdims=True)
            sg = (probs * (dpr - delta) * scale).astype(BF16)
            dk_acc[...] += jnp.dot(sg, q, preferred_element_type=F32)
            dv_acc[...] += jnp.dot(half, do, preferred_element_type=F32)
            return carry

        count = GROUP // wide
        cuts = (0, count // 4, count // 2, count)
        for first, last in zip(cuts, cuts[1:]):
            lax.fori_loop(first, last, chunk, 0, unroll=wide > 1)
            if between is not None and last < count:
                between()
        gs[h, :, 0] = dk_acc[...].astype(BF16).reshape(ctx_ways, toks, HEAD)
        gs[h, :, 1] = dv_acc[...].astype(BF16).reshape(ctx_ways, toks, HEAD)
        for step in range(1, ctx_ways):
            dst = lax.rem(ctx + step, ctx_ways)
            send(
                pltpu.make_async_remote_copy(
                    src_ref=gs.at[h, dst],
                    dst_ref=rs.at[h, ctx],
                    send_sem=g_send.at[h, step],
                    recv_sem=g_recv.at[h, ctx],
                    device_id=(dp, dst),
                    device_id_type=MESH,
                )
            )

    def grads(h):
        for step in range(1, ctx_ways):
            src = lax.rem(ctx + step, ctx_ways)
            pltpu.make_async_remote_copy(
                src_ref=gs.at[h, src],
                dst_ref=rs.at[h, src],
                send_sem=g_send.at[h, step],
                recv_sem=g_recv.at[h, src],
                device_id=(dp, src),
                device_id_type=MESH,
            ).wait_recv()
        pltpu.make_async_remote_copy(
            src_ref=wg.at[h],
            dst_ref=wo.at[h],
            send_sem=wo_send.at[h],
            recv_sem=wo_recv.at[h],
            device_id=(dp, partner),
            device_id_type=MESH,
        ).wait_recv()
        own = gs[h, ctx, core].astype(F32)
        cross = gs[h, ctx, 1 - core].astype(F32)
        for step in range(1, ctx_ways):
            src = lax.rem(ctx + step, ctx_ways)
            own += rs[h, src, core].astype(F32)
            cross += rs[h, src, 1 - core].astype(F32)
        return [own.astype(BF16), cross.astype(BF16)]

    def backward(heads):
        left = jnp.concatenate([g for h in heads for g in grads(h)], axis=1)
        row_total = jnp.zeros((toks, 1), F32)
        for p in range(dp_ways):
            cols = slice(p * rows, (p + 1) * rows)
            right = jnp.concatenate([w[h, p] for h in heads for w in (wg, wo)], axis=1)
            term = lax.dot_general(left, right, NT, preferred_element_type=F32)
            if heads[0] > 0:
                term += gn[:, cols]
            gn[:, cols] = term
            if heads[-1] == KV_HEADS - 1:
                row_total += jnp.sum(
                    emb_ref[:, cols].astype(F32) * gain_ref[:, cols] * term, axis=1, keepdims=True
                )
        return row_total

    relays_through(0)
    relays(2)
    complete(0)
    pltpu.make_async_remote_copy(
        src_ref=n2.at[1 - core],
        dst_ref=n2.at[1 - core],
        send_sem=n_send,
        recv_sem=n_recv,
        device_id=(dp, partner),
        device_id_type=MESH,
    ).wait_recv()
    for h in range(KV_HEADS):
        if h > 0:
            relays_through(h)
            complete(h)
        project(h)
        relays(2 if h == 0 else 1)
        if h == KV_HEADS - 1:
            backward(range(KV_HEADS // 2))
        attend(h, functools.partial(relays, 1))
    total = backward(range(KV_HEADS // 2, KV_HEADS))
    shift = inv_rms * inv_rms * inv_rms * (total * (1.0 / dim))
    for k in range(col_steps):
        cols = slice(k * step_cols, (k + 1) * step_cols)
        e = emb_ref[:, cols].astype(F32)
        out_ref[:, cols] = (inv_rms * gain_ref[:, cols] * gn[:, cols] - e * shift).astype(BF16)

    for copy, cond in sends:
        if cond is None:
            copy.wait_send()
        else:
            pl.when(cond)(copy.wait_send)


def body(embeds, norm_gain, w_key, w_value, queries, d_out, block_doc, slot_order):
    embed_rows = embeds[0]
    toks, dim = embed_rows.shape
    dp_ways = lax.axis_size("dp")
    ctx_ways = lax.axis_size("ctx")
    seq = toks * ctx_ways
    rows = dim // dp_ways
    vmem = pl.BlockSpec(memory_space=pltpu.VMEM)
    smem = pl.BlockSpec(memory_space=pltpu.SMEM)
    hbm = pl.BlockSpec(memory_space=pl.ANY)
    dma = pltpu.SemaphoreType.DMA
    splits = 2
    out = pl.pallas_call(
        functools.partial(kernel, dp_ways, ctx_ways),
        out_shape=jax.ShapeDtypeStruct((toks, dim), BF16),
        in_specs=[smem, smem, hbm, hbm, hbm, vmem, hbm, hbm],
        out_specs=vmem,
        scratch_shapes=[
            pltpu.VMEM((toks, dim), BF16),
            pltpu.VMEM((toks, dim), BF16),
            pltpu.VMEM((toks, dim), BF16),
            pltpu.VMEM((seq, toks), F32),
            dma((3,)),
            dma((KV_HEADS,)),
            pltpu.VMEM((KV_HEADS, dp_ways, rows, HEAD), BF16),
            pltpu.VMEM((KV_HEADS, dp_ways, rows, HEAD), BF16),
            pltpu.VMEM((2, toks, dim), BF16),
            pltpu.VMEM((2, KV_HEADS, ctx_ways, toks, HEAD), BF16),
            pltpu.VMEM((KV_HEADS, ctx_ways, 2, toks, HEAD), BF16),
            pltpu.VMEM((KV_HEADS, ctx_ways, 2, toks, HEAD), BF16),
            pltpu.VMEM((toks, dim), F32),
            pltpu.VMEM((seq, HEAD), F32),
            pltpu.VMEM((seq, HEAD), F32),
            dma((KV_HEADS, dp_ways, 4)),
            dma((KV_HEADS, dp_ways, splits)),
            dma,
            dma,
            dma((KV_HEADS,)),
            dma((KV_HEADS,)),
            dma((KV_HEADS, ctx_ways)),
            dma((KV_HEADS, ctx_ways)),
            dma((KV_HEADS, ctx_ways)),
            dma((KV_HEADS, ctx_ways)),
        ],
        compiler_params=pltpu.CompilerParams(
            collective_id=0, has_side_effects=True, vmem_limit_bytes=56 * 1024 * 1024
        ),
    )(
        block_doc, slot_order, w_key, w_value, embed_rows, norm_gain[None], queries[0], d_out[0]
    )
    return out[None]


def solution(mesh):
    in_specs = (
        P("dp", "ctx", None),
        P(),
        P("dp", None),
        P("dp", None),
        P("dp", "ctx", None),
        P("dp", "ctx", None),
        P("dp", None),
        P("dp", None),
    )
    out_specs = P("dp", "ctx", None)
    return jax.shard_map(body, mesh=mesh, in_specs=in_specs, out_specs=out_specs, check_vma=False)
```

```python
import functools
import math

import jax
import jax.numpy as jnp
from jax import lax
from jax.experimental import pallas as pl
from jax.experimental.pallas import tpu as pltpu
from jax.sharding import PartitionSpec as P

HEADS = 32
KV_HEADS = 4
HEAD = 128
GROUP = HEADS // KV_HEADS
DOC_BLOCK = 128
MESH = pl.DeviceIdType.MESH
F32 = jnp.float32
BF16 = jnp.bfloat16
NT = (((1,), (1,)), ((), ()))


def kernel(
    dp_ways,
    ctx_ways,
    doc_ref,
    slot_ref,
    wk_hbm,
    wv_hbm,
    emb_hbm,
    gain_ref,
    q_hbm,
    do_hbm,
    out_ref,
    emb_ref,
    q_ref,
    do_ref,
    bias_ref,
    load_sem,
    own_sem,
    wg,
    wo,
    n2,
    kv,
    gs,
    rs,
    gn,
    dk_acc,
    dv_acc,
    w_send,
    w_recv,
    n_send,
    n_recv,
    wo_send,
    wo_recv,
    kv_send,
    kv_recv,
    g_send,
    g_recv,
):
    toks, dim = emb_hbm.shape
    rows = dim // dp_ways
    line = dp_ways // 2
    chips = ctx_ways // 2
    splits = 2 if chips == 2 else 1
    part = rows // splits
    seq = toks * ctx_ways

    dp = lax.axis_index("dp")
    ctx = lax.axis_index("ctx")
    za, yb = dp // 2, dp % 2
    chip, core = ctx // 2, ctx % 2
    mine = chip % splits
    other = splits - 1 - mine
    partner = chip * 2 + 1 - core
    y_dp = za * 2 + 1 - yb
    x_ctx = (chips - 1 - chip) * 2 + core
    has_up, has_down = za + 1 < line, za >= 1
    sends = []

    def send(copy, cond=None):
        if cond is None:
            copy.start()
        else:
            pl.when(cond)(copy.start)
        sends.append((copy, cond))

    barrier = pltpu.get_barrier_semaphore()

    def greet(where):
        pl.semaphore_signal(barrier, inc=1, device_id=where, device_id_type=MESH)

    for step in range(1, ctx_ways):
        greet((dp, lax.rem(ctx + step, ctx_ways)))
    greet((y_dp, ctx))
    pl.when(has_up)(lambda: greet((dp + 2, ctx)))
    pl.when(has_down)(lambda: greet((dp - 2, ctx)))

    def own_load(src, h):
        return pltpu.make_async_copy(
            src.at[:, pl.ds(h * HEAD, HEAD)], wg.at[h, dp], own_sem.at[h]
        )

    for h in range(KV_HEADS):
        pl.when(core == 0)(own_load(wk_hbm, h).start)
        pl.when(core == 1)(own_load(wv_hbm, h).start)
    loads = [
        pltpu.make_async_copy(src, dst, load_sem.at[i])
        for i, (src, dst) in enumerate(((emb_hbm, emb_ref), (q_hbm, q_ref), (do_hbm, do_ref)))
    ]
    for load in loads:
        load.start()

    pl.semaphore_wait(
        barrier, ctx_ways + jnp.where(has_up, 1, 0) + jnp.where(has_down, 1, 0)
    )

    up, down, ybor, xbor = (dp + 2, ctx), (dp - 2, ctx), (y_dp, ctx), (dp, x_ctx)

    def w_copy(h, p, s, slot, where):
        if s is None:
            ref, sem = wg.at[h, p], 0
        else:
            ref, sem = wg.at[h, p, pl.ds(pl.multiple_of(s * part, part), part)], s
        return pltpu.make_async_remote_copy(
            src_ref=ref,
            dst_ref=ref,
            send_sem=w_send.at[h, p, slot],
            recv_sem=w_recv.at[h, p, sem],
            device_id=where,
            device_id_type=MESH,
        )

    def arrive(h, p, s, cond):
        @pl.when(cond)
        def _():
            w_copy(h, p, s, 0, up).wait_recv()

    def start_own(h):
        own_load(wk_hbm, h).wait()
        send(w_copy(h, dp, None, 0, up), has_up)
        send(w_copy(h, dp, None, 1, down), has_down)
        send(w_copy(h, dp, None, 2, ybor))

    def sides(d):
        odd = za % 2 == 1
        never = za < 0
        return (
            (-2 * d, za >= d, odd if d == 1 else never, 1),
            (2 * d, za + d < line, jnp.logical_not(odd) if d == 1 else never, 0),
        )

    def relay(h, k):
        if k < line:
            for off, inside, whole, away in sides(k):
                p = dp + off
                arrive(h, p, None, inside)
                if away == 1:
                    send(w_copy(h, p, None, 0, up), inside & has_up)
                else:
                    send(w_copy(h, p, None, 1, down), inside & has_down)
                if splits == 1:
                    send(w_copy(h, p, None, 2, ybor), inside)
                else:
                    if k == 1:
                        send(w_copy(h, p, None, 2, ybor), inside & whole)
                    send(
                        w_copy(h, p, mine, 2, ybor),
                        inside & jnp.logical_not(whole) if k == 1 else inside,
                    )
        if k > 1 and splits == 2:
            for off, inside, whole, _away in sides(k - 1):
                p = y_dp + off
                half = inside & jnp.logical_not(whole) if k == 2 else inside
                arrive(h, p, mine, half)
                send(w_copy(h, p, mine, 3, xbor), half)

    def complete(h):
        w_copy(h, y_dp, None, 0, up).wait_recv()
        for d in range(1, line):
            for off, inside, whole, _away in sides(d):
                p = y_dp + off
                if splits == 1:
                    arrive(h, p, None, inside)
                elif d == 1:
                    arrive(h, p, None, inside & whole)
                    arrive(h, p, other, inside & jnp.logical_not(whole))
                else:
                    arrive(h, p, other, inside)

    steps = [
        (h, w - h + 1)
        for w in range(KV_HEADS + line - 1)
        for h in range(KV_HEADS)
        if 1 <= w - h + 1 <= line
    ]

    def relays(count):
        for _ in range(min(count, len(steps))):
            h, k = steps.pop(0)
            if k == 1 and h + 1 < KV_HEADS:
                start_own(h + 1)
            relay(h, k)

    def relays_through(h):
        if (h, line) in steps:
            relays(steps.index((h, line)) + 1)

    start_own(0)
    loads[0].wait()

    step_cols = 512
    col_steps = dim // step_cols
    total = jnp.zeros((toks, 1), F32)
    for k in range(col_steps):
        e = emb_ref[:, k * step_cols : (k + 1) * step_cols].astype(F32)
        total += jnp.sum(e * e, axis=1, keepdims=True)
    inv_rms = lax.rsqrt(total * (1.0 / dim) + 1e-05)
    relays(1)
    for k in range(col_steps):
        cols = slice(k * step_cols, (k + 1) * step_cols)
        e = emb_ref[:, cols].astype(F32)
        n2[core, :, cols] = (e * inv_rms * gain_ref[:, cols]).astype(BF16)
    n_copy = pltpu.make_async_remote_copy(
        src_ref=n2.at[core],
        dst_ref=n2.at[core],
        send_sem=n_send,
        recv_sem=n_recv,
        device_id=(dp, partner),
        device_id_type=MESH,
    )
    send(n_copy)

    slots = slot_ref.shape[1]
    half_len = seq // slots
    lane = lax.broadcasted_iota(jnp.int32, (1, toks), 1)
    down_rows = lax.broadcasted_iota(jnp.int32, (half_len, 1), 0)
    per_dev = toks // half_len

    def slot_doc(start):
        block, found = start // DOC_BLOCK, jnp.int32(0)
        for i in range(doc_ref.shape[1]):
            found = jnp.where(block == i, doc_ref[0, i], found)
        return found

    q_pos = jnp.zeros((1, toks), jnp.int32)
    q_doc = jnp.zeros((1, toks), jnp.int32)
    for i in range(per_dev):
        start = slot_ref[0, ctx * per_dev + i] * half_len
        here = (lane >= i * half_len) & (lane < (i + 1) * half_len)
        q_pos = jnp.where(here, start + lane - i * half_len, q_pos)
        q_doc = jnp.where(here, slot_doc(start), q_doc)
    for j in range(slots):
        start = slot_ref[0, j] * half_len
        allowed = ((start + down_rows) <= q_pos) & (q_doc == slot_doc(start))
        bias_ref[j * half_len : (j + 1) * half_len, :] = jnp.where(allowed, 0.0, -jnp.inf)

    def project(h):
        acc = jnp.zeros((2 * toks, HEAD), F32)
        for p in range(dp_ways):
            x = n2[:, :, p * rows : (p + 1) * rows].reshape(2 * toks, rows)
            acc += jnp.dot(x, wg[h, p], preferred_element_type=F32)
        kv[core, h, pl.ds(chip * 2, 2)] = acc.astype(BF16).reshape(2, toks, HEAD)
        for step in range(1, ctx_ways):
            send(
                pltpu.make_async_remote_copy(
                    src_ref=kv.at[core, h, pl.ds(chip * 2, 2)],
                    dst_ref=kv.at[core, h, pl.ds(chip * 2, 2)],
                    send_sem=kv_send.at[h, step],
                    recv_sem=kv_recv.at[h, ctx],
                    device_id=(dp, lax.rem(ctx + step, ctx_ways)),
                    device_id_type=MESH,
                )
            )
        send(
            pltpu.make_async_remote_copy(
                src_ref=wg.at[h],
                dst_ref=wo.at[h],
                send_sem=wo_send.at[h],
                recv_sem=wo_recv.at[h],
                device_id=(dp, partner),
                device_id_type=MESH,
            )
        )

    wide = 2 if seq <= 512 else 1
    scale = HEAD ** (-0.5)

    def attend(h, between=None):
        for step in range(1, ctx_ways):
            src = lax.rem(ctx + step, ctx_ways)
            at = (src // 2) * 2
            blk = kv.at[src % 2, h, pl.ds(at, 2)]
            pltpu.make_async_remote_copy(
                src_ref=blk,
                dst_ref=blk,
                send_sem=kv_send.at[h, step],
                recv_sem=kv_recv.at[h, src],
                device_id=(dp, src),
                device_id_type=MESH,
            ).wait_recv()
        dk_acc[...] = jnp.zeros_like(dk_acc)
        dv_acc[...] = jnp.zeros_like(dv_acc)
        if h == 0:
            loads[1].wait()
            loads[2].wait()

        def chunk(i, carry):
            first = (h * GROUP + i * wide) * HEAD

            def take(ref):
                cuts = [
                    ref[:, pl.ds(pl.multiple_of(first + w * HEAD, HEAD), HEAD)]
                    for w in range(wide)
                ]
                return jnp.concatenate(cuts, axis=0) if wide > 1 else cuts[0]

            q, do = take(q_ref), take(do_ref)
            keys = kv[0, h].reshape(seq, HEAD)
            vals = kv[1, h].reshape(seq, HEAD)
            bias = bias_ref[...]
            if wide > 1:
                bias = jnp.concatenate([bias] * wide, axis=1)
            s = lax.dot_general(keys, q, NT, preferred_element_type=F32) + bias
            top = jnp.max(s, axis=0, keepdims=True)
            raised = jnp.exp2((s - top) * (scale * math.log2(math.e)))
            probs = raised * (1.0 / jnp.sum(raised, axis=0, keepdims=True))
            half = probs.astype(BF16)
            dpr = lax.dot_general(vals, do, NT, preferred_element_type=F32)
            delta = jnp.sum(half.astype(F32) * dpr, axis=0, keepdims=True)
            sg = (probs * (dpr - delta) * scale).astype(BF16)
            dk_acc[...] += jnp.dot(sg, q, preferred_element_type=F32)
            dv_acc[...] += jnp.dot(half, do, preferred_element_type=F32)
            return carry

        count = GROUP // wide
        cuts = (0, count // 4, count // 2, count)
        for first, last in zip(cuts, cuts[1:]):
            lax.fori_loop(first, last, chunk, 0, unroll=wide > 1)
            if between is not None and last < count:
                between()
        gs[h, :, 0] = dk_acc[...].astype(BF16).reshape(ctx_ways, toks, HEAD)
        gs[h, :, 1] = dv_acc[...].astype(BF16).reshape(ctx_ways, toks, HEAD)
        for step in range(1, ctx_ways):
            dst = lax.rem(ctx + step, ctx_ways)
            send(
                pltpu.make_async_remote_copy(
                    src_ref=gs.at[h, dst],
                    dst_ref=rs.at[h, ctx],
                    send_sem=g_send.at[h, step],
                    recv_sem=g_recv.at[h, ctx],
                    device_id=(dp, dst),
                    device_id_type=MESH,
                )
            )

    def grads(h):
        for step in range(1, ctx_ways):
            src = lax.rem(ctx + step, ctx_ways)
            pltpu.make_async_remote_copy(
                src_ref=gs.at[h, src],
                dst_ref=rs.at[h, src],
                send_sem=g_send.at[h, step],
                recv_sem=g_recv.at[h, src],
                device_id=(dp, src),
                device_id_type=MESH,
            ).wait_recv()
        pltpu.make_async_remote_copy(
            src_ref=wg.at[h],
            dst_ref=wo.at[h],
            send_sem=wo_send.at[h],
            recv_sem=wo_recv.at[h],
            device_id=(dp, partner),
            device_id_type=MESH,
        ).wait_recv()
        own = gs[h, ctx, core].astype(F32)
        cross = gs[h, ctx, 1 - core].astype(F32)
        for step in range(1, ctx_ways):
            src = lax.rem(ctx + step, ctx_ways)
            own += rs[h, src, core].astype(F32)
            cross += rs[h, src, 1 - core].astype(F32)
        return [own.astype(BF16), cross.astype(BF16)]

    def backward(heads):
        left = jnp.concatenate([g for h in heads for g in grads(h)], axis=1)
        row_total = jnp.zeros((toks, 1), F32)
        for p in range(dp_ways):
            cols = slice(p * rows, (p + 1) * rows)
            right = jnp.concatenate([w[h, p] for h in heads for w in (wg, wo)], axis=1)
            term = lax.dot_general(left, right, NT, preferred_element_type=F32)
            if heads[0] > 0:
                term += gn[:, cols]
            gn[:, cols] = term
            if heads[-1] == KV_HEADS - 1:
                row_total += jnp.sum(
                    emb_ref[:, cols].astype(F32) * gain_ref[:, cols] * term, axis=1, keepdims=True
                )
        return row_total

    relays_through(0)
    relays(2)
    complete(0)
    pltpu.make_async_remote_copy(
        src_ref=n2.at[1 - core],
        dst_ref=n2.at[1 - core],
        send_sem=n_send,
        recv_sem=n_recv,
        device_id=(dp, partner),
        device_id_type=MESH,
    ).wait_recv()
    for h in range(KV_HEADS):
        if h > 0:
            relays_through(h)
            complete(h)
        project(h)
        relays(2 if h == 0 else 1)
        if h == KV_HEADS - 1:
            backward(range(KV_HEADS // 2))
        attend(h, functools.partial(relays, 1))
    total = backward(range(KV_HEADS // 2, KV_HEADS))
    shift = inv_rms * inv_rms * inv_rms * (total * (1.0 / dim))
    for k in range(col_steps):
        cols = slice(k * step_cols, (k + 1) * step_cols)
        e = emb_ref[:, cols].astype(F32)
        out_ref[:, cols] = inv_rms * gain_ref[:, cols] * gn[:, cols] - e * shift

    for copy, cond in sends:
        if cond is None:
            copy.wait_send()
        else:
            pl.when(cond)(copy.wait_send)


def body(embeds, norm_gain, w_key, w_value, queries, d_out, block_doc, slot_order):
    embed_rows = embeds[0]
    toks, dim = embed_rows.shape
    dp_ways = lax.axis_size("dp")
    ctx_ways = lax.axis_size("ctx")
    seq = toks * ctx_ways
    rows = dim // dp_ways
    vmem = pl.BlockSpec(memory_space=pltpu.VMEM)
    smem = pl.BlockSpec(memory_space=pltpu.SMEM)
    hbm = pl.BlockSpec(memory_space=pl.ANY)
    dma = pltpu.SemaphoreType.DMA
    splits = 2
    out = pl.pallas_call(
        functools.partial(kernel, dp_ways, ctx_ways),
        out_shape=jax.ShapeDtypeStruct((toks, dim), F32),
        in_specs=[smem, smem, hbm, hbm, hbm, vmem, hbm, hbm],
        out_specs=vmem,
        scratch_shapes=[
            pltpu.VMEM((toks, dim), BF16),
            pltpu.VMEM((toks, dim), BF16),
            pltpu.VMEM((toks, dim), BF16),
            pltpu.VMEM((seq, toks), F32),
            dma((3,)),
            dma((KV_HEADS,)),
            pltpu.VMEM((KV_HEADS, dp_ways, rows, HEAD), BF16),
            pltpu.VMEM((KV_HEADS, dp_ways, rows, HEAD), BF16),
            pltpu.VMEM((2, toks, dim), BF16),
            pltpu.VMEM((2, KV_HEADS, ctx_ways, toks, HEAD), BF16),
            pltpu.VMEM((KV_HEADS, ctx_ways, 2, toks, HEAD), BF16),
            pltpu.VMEM((KV_HEADS, ctx_ways, 2, toks, HEAD), BF16),
            pltpu.VMEM((toks, dim), F32),
            pltpu.VMEM((seq, HEAD), F32),
            pltpu.VMEM((seq, HEAD), F32),
            dma((KV_HEADS, dp_ways, 4)),
            dma((KV_HEADS, dp_ways, splits)),
            dma,
            dma,
            dma((KV_HEADS,)),
            dma((KV_HEADS,)),
            dma((KV_HEADS, ctx_ways)),
            dma((KV_HEADS, ctx_ways)),
            dma((KV_HEADS, ctx_ways)),
            dma((KV_HEADS, ctx_ways)),
        ],
        compiler_params=pltpu.CompilerParams(
            collective_id=0, has_side_effects=True, vmem_limit_bytes=56 * 1024 * 1024
        ),
    )(
        block_doc, slot_order, w_key, w_value, embed_rows, norm_gain[None], queries[0], d_out[0]
    )
    return out.astype(BF16)[None]


def solution(mesh):
    in_specs = (
        P("dp", "ctx", None),
        P(),
        P("dp", None),
        P("dp", None),
        P("dp", "ctx", None),
        P("dp", "ctx", None),
        P("dp", None),
        P("dp", None),
    )
    out_specs = P("dp", "ctx", None)
    return jax.shard_map(body, mesh=mesh, in_specs=in_specs, out_specs=out_specs, check_vma=False)
```
